256 devices in a mesh: dp: 16 (over z, x_lo), frame: 16 (over x_hi, y, core).
Axes of the slice: x: 4 (x_hi: 2, x_lo: 2; x = x_hi * 2 + x_lo), y: 4, z: 8, core: 2. Of those that a mesh axis runs over, the one named last changes fastest.
Arguments:
- latents: bfloat16 [16, 16, 8, 16, 1280], P('dp', 'frame'), may hold values from -6 to 6
- out_grad: bfloat16 [16, 16, 8, 16, 1280], P('dp', 'frame'), may hold values from -6 to 6
- video: bfloat16 [16, 16, 16, 32, 1280], P('dp', 'frame'), may hold values from -6 to 6
- owner: int32 [16], P('dp'), may hold values from 0 to 15
- w_query: bfloat16 [1280, 640], replicated, may hold values from -0.15625 to 0.15625
- w_key: bfloat16 [1280, 640], replicated, may hold values from -0.15625 to 0.15625
- w_value: bfloat16 [1280, 640], replicated, may hold values from -0.15625 to 0.15625
- w_out: bfloat16 [640, 1280], replicated, may hold values from -0.25 to 0.25
Outputs:
- block_out: bfloat16 [16, 16, 8, 16, 1280], P('dp', 'frame')
- grad_latents: bfloat16 [16, 16, 8, 16, 1280], P('dp', 'frame')
- grad_weights: float32 [1280, 1280], P(('dp', 'frame'))
The draws below stay inside these ranges and needn't reach their ends.
Inputs may be any that keep to these rules, and one draw needn't show every extreme that they name: owner[o] is the frame index of the device whose video slot holds object o's input video.
All inputs are finite; a program needn't handle non-finite values.
Results may differ from the reference program's by a relative error of at most 0.013.
Values may be sent and summed in bfloat16 or wider, within the bound.
A program may use at most 128 MiB of HBM per device.

```python
import jax
import jax.numpy as jnp
from jax import lax

D = 1280
HEADS = 10
HD = 64
VIEWS = 8
PATCH = 16
VT = 32
INNER = 640
ROWS = 128
FRAMES = 16
OBJECTS = 16
N_FRAME = 16


def place_ends(entries, rng, low, top_value):
    longest = entries.shape.index(max(entries.shape))
    spots = []
    for shift in (0, 1):
        where = [jax.random.randint(jax.random.fold_in(rng, axis), (), 0, length) for axis, length in enumerate(entries.shape)]
        where[longest] = (where[longest] + shift) % entries.shape[longest]
        spots.append(tuple(where))
    return entries.at[spots[0]].set(low).at[spots[1]].set(top_value)


def block_scale(own_key, shape, cuts, least, top_value):
    loudness = 1.0
    for dim, blocks in cuts:
        draws = jax.random.uniform(jax.random.fold_in(jax.random.fold_in(own_key, 6), dim), (blocks,), jnp.float32, least / len(cuts), top_value / len(cuts))
        loudness = loudness * jnp.repeat(jnp.exp(draws), shape[dim] // blocks).reshape((-1,) + (1,) * (len(shape) - 1 - dim))
    return loudness


def gaussian(own_key, extent, scale, reach, shards=(), held_as=jnp.bfloat16):
    values = scale * jax.random.normal(own_key, extent, jnp.float32)
    if shards:
        values = values * block_scale(own_key, extent, shards, -0.22, 0.18)
    return jnp.clip(values, -reach, reach).astype(held_as)


def setup_inputs(seed: int = 0) -> dict:
    splits = jax.random.split(jax.random.key(seed), 9)
    return {
        "latents": gaussian(splits[0], (OBJECTS, FRAMES, VIEWS, PATCH, D), 1.0, 6.0, ((0, 16), (1, 16))),
        "out_grad": gaussian(splits[1], (OBJECTS, FRAMES, VIEWS, PATCH, D), 1.0, 6.0, ((0, 16), (1, 16))),
        "video": gaussian(splits[2], (OBJECTS, FRAMES, FRAMES, VT, D), 1.0, 6.0, ((0, 16), (1, 16))),
        "owner": place_ends(jax.random.randint(splits[3], (OBJECTS,), 0, N_FRAME), jax.random.fold_in(splits[3], 1), 0, N_FRAME - 1).astype(jnp.int32),
        "w_query": gaussian(splits[4], (D, INNER), D ** -0.5, 0.15625),
        "w_key": gaussian(splits[5], (D, INNER), D ** -0.5, 0.15625),
        "w_value": gaussian(splits[6], (D, INNER), D ** -0.5, 0.15625),
        "w_out": gaussian(splits[7], (INNER, D), INNER ** -0.5, 0.25),
    }


def normalize(tensor):
    factor = lax.rsqrt(lax.optimization_barrier(jnp.mean(tensor * tensor, axis=-1, keepdims=True)) + 1e-06)
    return (tensor * factor, factor)

def to_half(tensor):
    return lax.optimization_barrier(tensor.astype(jnp.bfloat16)).astype(jnp.float32)

def reference(latents, out_grad, video, owner, w_query, w_key, w_value, w_out):
    inv = HD ** (-0.5)

    def one_object(total, inputs):
        latent, cotangent, slots, who = inputs
        xf = latent.reshape(FRAMES * ROWS, D).astype(jnp.float32)
        normed, factor = normalize(xf)
        xn = normed.astype(jnp.bfloat16)
        cond = lax.dynamic_index_in_dim(slots, who, 0, keepdims=False)
        cn = normalize(cond.reshape(FRAMES * VT, D).astype(jnp.float32))[0].astype(jnp.bfloat16)
        query = jnp.dot(xn, w_query, preferred_element_type=jnp.float32).astype(jnp.bfloat16)
        key = jnp.dot(xn, w_key, preferred_element_type=jnp.float32).astype(jnp.bfloat16)
        value = jnp.dot(xn, w_value, preferred_element_type=jnp.float32).astype(jnp.bfloat16)
        key_c = jnp.dot(cn, w_key, preferred_element_type=jnp.float32).astype(jnp.bfloat16)
        value_c = jnp.dot(cn, w_value, preferred_element_type=jnp.float32).astype(jnp.bfloat16)
        q4 = query.reshape(FRAMES, ROWS, HEADS, HD).astype(jnp.float32)
        k4 = key.reshape(FRAMES, ROWS, HEADS, HD).astype(jnp.float32)
        v4 = value.reshape(FRAMES, ROWS, HEADS, HD).astype(jnp.float32)
        keys = jnp.concatenate([k4, key_c.reshape(FRAMES, VT, HEADS, HD).astype(jnp.float32)], axis=1)
        vals = jnp.concatenate([v4, value_c.reshape(FRAMES, VT, HEADS, HD).astype(jnp.float32)], axis=1)
        score = jnp.einsum('frhd,fkhd->fhrk', q4, keys) * inv
        expo = jnp.exp(score)
        tot = lax.optimization_barrier(jnp.sum(expo, axis=-1))
        view_out = jnp.einsum('fhrk,fkhd->frhd', to_half(expo), vals) / jnp.transpose(tot, (0, 2, 1))[..., None]
        tscore = jnp.einsum('frhd,grhd->rhfg', q4, k4) * inv
        texpo = jnp.exp(tscore)
        ttot = lax.optimization_barrier(jnp.sum(texpo, axis=-1))
        time_out = jnp.einsum('rhfg,grhd->frhd', to_half(texpo), v4) / jnp.transpose(ttot, (2, 0, 1))[..., None]
        hidden = (view_out + time_out).reshape(FRAMES * ROWS, INNER).astype(jnp.bfloat16)
        block = (xf + jnp.dot(hidden, w_out, preferred_element_type=jnp.float32)).astype(jnp.bfloat16)
        grad_y = cotangent.reshape(FRAMES * ROWS, D)
        go = jnp.dot(grad_y, w_out.T, preferred_element_type=jnp.float32).astype(jnp.bfloat16)
        go4 = go.reshape(FRAMES, ROWS, HEADS, HD).astype(jnp.float32)
        prob = expo / tot[..., None]
        dval = jnp.einsum('fhrk,frhd->fkhd', to_half(prob), go4)
        dprob = jnp.einsum('frhd,fkhd->fhrk', go4, vals)
        delta = jnp.transpose(lax.optimization_barrier(jnp.sum(go4 * view_out, axis=-1)), (0, 2, 1))
        dscore = to_half(prob * (dprob - delta[..., None]))
        dq_view = jnp.einsum('fhrk,fkhd->frhd', dscore, keys) * inv
        dkey = jnp.einsum('fhrk,frhd->fkhd', dscore, q4) * inv
        tprob = texpo / ttot[..., None]
        dtprob = jnp.einsum('frhd,grhd->rhfg', go4, v4)
        tdelta = jnp.transpose(lax.optimization_barrier(jnp.sum(go4 * time_out, axis=-1)), (1, 2, 0))
        dts = tprob * (dtprob - tdelta[..., None])
        dq_time = jnp.einsum('rhfg,grhd->frhd', dts, k4) * inv
        dk_time = lax.optimization_barrier(jnp.sum(to_half(jnp.einsum('rhfg,frhd->fgrhd', dts, q4) * inv), axis=0))
        dv_time = lax.optimization_barrier(jnp.sum(to_half(jnp.einsum('rhfg,frhd->fgrhd', tprob, go4)), axis=0))
        dq = (dq_view + dq_time).reshape(FRAMES * ROWS, INNER).astype(jnp.bfloat16)
        dk = (dkey[:, :ROWS] + dk_time).reshape(FRAMES * ROWS, INNER).astype(jnp.bfloat16)
        dv = (dval[:, :ROWS] + dv_time).reshape(FRAMES * ROWS, INNER).astype(jnp.bfloat16)
        dkc = dkey[:, ROWS:].reshape(FRAMES * VT, INNER).astype(jnp.bfloat16)
        dvc = dval[:, ROWS:].reshape(FRAMES * VT, INNER).astype(jnp.bfloat16)
        grad_k = jnp.dot(xn.T, dk, preferred_element_type=jnp.float32) + jnp.dot(cn.T, dkc, preferred_element_type=jnp.float32)
        grad_v = jnp.dot(xn.T, dv, preferred_element_type=jnp.float32) + jnp.dot(cn.T, dvc, preferred_element_type=jnp.float32)
        dnorm = jnp.dot(dq, w_query.T, preferred_element_type=jnp.float32)
        dnorm = dnorm + jnp.dot(dk, w_key.T, preferred_element_type=jnp.float32)
        dnorm = dnorm + jnp.dot(dv, w_value.T, preferred_element_type=jnp.float32)
        back = grad_y.astype(jnp.float32) + factor * (dnorm - normed * lax.optimization_barrier(jnp.mean(dnorm * normed, axis=-1, keepdims=True)))
        total = total + jnp.concatenate([grad_k, grad_v], axis=1)
        shaped = (FRAMES, VIEWS, PATCH, D)
        return (total, (block.reshape(shaped), back.astype(jnp.bfloat16).reshape(shaped)))
    start = jnp.zeros((D, 2 * INNER), jnp.float32)
    total, outs = lax.scan(one_object, start, (latents, out_grad, video, owner.astype(jnp.int32)))
    return (outs[0], outs[1], total)
```

```python
import jax
import jax.numpy as jnp
from jax import lax
from jax.experimental import pallas as pl
from jax.experimental.pallas import tpu as pltpu
from jax.sharding import PartitionSpec as P

MESH = pl.DeviceIdType.MESH
BF = jnp.bfloat16
F32 = jnp.float32
D, INNER, HD = 1280, 640, 64
ROWS, VT, NF = 128, 32, 16
KEYS = 256
EPS = 1e-6
CHUNKS = ((0, 2), (2, 5))
NC = len(CHUNKS)


def nn(a, b):
    return jnp.dot(a, b, preferred_element_type=F32)


def nt(a, b):
    return lax.dot_general(a, b, (((1,), (1,)), ((), ())), preferred_element_type=F32)


def tn(a, b):
    return lax.dot_general(a, b, (((0,), (0,)), ((), ())), preferred_element_type=F32)


def attend(q, k, v, go, mask):
    lane = lax.broadcasted_iota(jnp.int32, (1, 128), 1)
    first = (lane < HD).astype(F32).astype(BF)
    second = (lane >= HD).astype(F32).astype(BF)
    qm = jnp.concatenate([q * first, q * second], axis=0)
    gm = jnp.concatenate([go * first, go * second], axis=0)
    km = jnp.concatenate([k * first, k * second], axis=0)
    vm = jnp.concatenate([v * first, v * second], axis=0)
    e = jnp.where(mask, jnp.exp(nt(qm, k) * 0.125), 0.0)
    dp = nt(gm, v)
    r = 1.0 / jnp.sum(e, axis=1, keepdims=True)
    eb = e.astype(BF)
    o = nn(jnp.concatenate([eb[:ROWS], eb[ROWS:]], axis=1), vm)
    o = o * jnp.where(lane < HD, r[:ROWS], r[ROWS:])
    delta = jnp.sum(gm.astype(F32) * jnp.concatenate([o, o], axis=0), axis=1, keepdims=True)
    p = e * r
    ds = (p * (dp - delta)).astype(BF)
    dq = nn(jnp.concatenate([ds[:ROWS], ds[ROWS:]], axis=1), km) * 0.125
    dk = tn(ds, qm) * 0.125
    dv = tn(p.astype(BF), gm)
    return o, dq, dk, dv


def pack(top, bottom):
    return jnp.concatenate([top.reshape(NF, 8, 128), bottom.reshape(NF, 8, 128)], axis=1).astype(BF)


def unpack(block):
    wide = block.astype(F32)
    return wide[:, :8].reshape(ROWS, 128), wide[:, 8:].reshape(ROWS, 128)


def kernel(
    lat, ogr, vid, own, wq_h, wk_h, wv_h, wo_h,
    block_h, back_h, grad_o,
    lat_v, ogr_v, wq, wk, wv, wo, block_v, back_v,
    normed, xc, q_v, kk, vv, go_v, snd, rcv, snd2, rcv2,
    va, vb, vs, vy, v2, vx,
    ov, dqv, dkv_v, dvv_v, h_v, dq_b, dkv,
    pt, gx, gy, rx, ry, s2x, s2y, r2x, r2y, m1, s3, r3,
    load_sem, as1, ar1, as2, ar2, ms, mr,
):
    dp = lax.axis_index("dp")
    me = lax.axis_index("frame")
    z, x_lo = dp // 2, dp % 2
    x_hi, y, c = me // 8, (me // 2) % 4, me % 2
    x = x_hi * 2 + x_lo

    def at_x(d):
        to = (x + d) % 4
        return (z * 2 + to % 2, (to // 2) * 8 + y * 2 + c)

    def at_y(d):
        return (dp, x_hi * 8 + ((y + d) % 4) * 2 + c)

    def at_z(d):
        return (((z + d) % 8) * 2 + x_lo, me)

    def at_f(d):
        return (dp, (me + d) % NF)

    pair = (dp, me + 1 - 2 * c)

    loads = [
        pltpu.make_async_copy(src, dst, load_sem.at[i])
        for i, (src, dst) in enumerate(
            [(lat, lat_v), (wq_h, wq), (wk_h, wk), (wv_h, wv), (ogr, ogr_v), (wo_h, wo), (vid.at[:, c], va)]
        )
    ]
    for copy in loads:
        copy.start()

    barrier = pltpu.get_barrier_semaphore()
    peers = [at_f(d) for d in range(1, NF)] + [at_x(1), at_x(3)] + [at_z(d) for d in range(1, 8)]
    for peer in peers:
        pl.semaphore_signal(barrier, inc=1, device_id=peer, device_id_type=MESH)

    count = [0]
    started = []

    def send(src, dst, peer, ss=None, rs=None):
        if ss is None:
            ss, rs = ms.at[count[0]], mr.at[count[0]]
            count[0] += 1
        copy = pltpu.make_async_remote_copy(
            src_ref=src, dst_ref=dst, send_sem=ss, recv_sem=rs, device_id=peer, device_id_type=MESH
        )
        copy.start()
        started.append(copy)
        return copy

    def arrived(dst, rs):
        pltpu.make_async_remote_copy(
            src_ref=dst, dst_ref=dst, send_sem=rs, recv_sem=rs, device_id=pair, device_id_type=MESH
        ).wait_recv()

    loads[0].wait()
    xf = lat_v[...].astype(F32)
    factor = lax.rsqrt(jnp.mean(xf * xf, axis=1, keepdims=True) + EPS)
    norm = xf * factor
    normed[...] = norm
    xn = norm.astype(BF)
    xc[0, :ROWS] = xn

    pl.semaphore_wait(barrier, len(peers))
    core_copy = send(vid.at[:, 1 - c], vb, pair)
    xn_copy = send(xc.at[0, pl.ds(0, ROWS)], xc.at[1, pl.ds(0, ROWS)], pair)

    for copy in loads[1:6]:
        copy.wait()
    grad_y = ogr_v[...]
    for n, (a, b) in enumerate(CHUNKS):
        cols = slice(a * 128, b * 128)
        qf = nn(xn, wq[:, cols])
        kf = nn(xn, wk[:, cols])
        vf = nn(xn, wv[:, cols])
        gf = nt(grad_y, wo[cols, :])
        for p in range(a, b):
            part = slice((p - a) * 128, (p - a + 1) * 128)
            snd[:, :, p * 256 : p * 256 + 128] = pack(qf[:, part], vf[:, part])
            snd[:, :, p * 256 + 128 : p * 256 + 256] = pack(kf[:, part], gf[:, part])
        lanes = pl.ds(a * 256, (b - a) * 256)
        for d in range(1, NF):
            to = (me + d) % NF
            send(snd.at[to, :, lanes], rcv.at[me, :, lanes], at_f(d), as1.at[n, d], ar1.at[n, d])
        q_v[:, cols] = qf.astype(BF)
        kk[:ROWS, cols] = kf.astype(BF)
        vv[:ROWS, cols] = vf.astype(BF)
        go_v[:, cols] = gf.astype(BF)
    rcv[me] = snd[me]

    who = own[0]
    loads[6].wait()
    core_copy.wait_recv()
    w = (who % 2 == c).astype(F32)
    vs[...] = (va[...].astype(F32) * w + vb[...].astype(F32) * (1.0 - w)).astype(BF).reshape(2, 4, VT, D)
    y_copies = [send(vs.at[:, (y + d) % 4], vy.at[d - 1], at_y(d)) for d in range(1, 4)]

    new = lax.broadcasted_iota(jnp.int32, (INNER, 1), 0)
    u = (new * 52429) >> 18
    k5 = new - 5 * u
    uz, lo, hi = u & 7, (u >> 3) & 3, u >> 5
    column = lax.broadcasted_iota(jnp.int32, (1, D), 1)

    def one_hot(ux, uy):
        old = ((((uz * 2 + (ux & 1)) * 2 + (ux >> 1)) * 4 + uy) * 2 + c) * 5 + k5
        return (old == column).astype(F32).astype(BF)

    pt[0] = one_hot(hi, lo)
    pt[1] = one_hot(lo, hi)
    xn_copy.wait_recv()

    same = (
        (lax.broadcasted_iota(jnp.int32, (2 * ROWS, ROWS), 0) - lax.broadcasted_iota(jnp.int32, (2 * ROWS, ROWS), 1)) & 7
    ) == 0
    for n, (a, b) in enumerate(CHUNKS):
        lanes = pl.ds(a * 256, (b - a) * 256)
        for d in range(1, NF):
            arrived(rcv.at[(me + NF - d) % NF, :, lanes], ar1.at[n, d])
        for p in range(a, b):
            q, v = unpack(rcv[:, :, p * 256 : p * 256 + 128])
            k, go = unpack(rcv[:, :, p * 256 + 128 : p * 256 + 256])
            o, dq, dk, dv = attend(q.astype(BF), k.astype(BF), v.astype(BF), go.astype(BF), same)
            snd2[:, :, p * 256 : p * 256 + 128] = pack(o, dk)
            snd2[:, :, p * 256 + 128 : p * 256 + 256] = pack(dq, dv)
        for d in range(1, NF):
            to = (me + d) % NF
            send(snd2.at[to, :, lanes], rcv2.at[me, :, lanes], at_f(d), as2.at[n, d], ar2.at[n, d])
        if n == 0:
            oy = (who // 2) % 4
            total = vs[:, y].astype(F32) * (oy == y).astype(F32)
            for d in range(1, 4):
                y_copies[d - 1].wait_recv()
                total = total + vy[d - 1].astype(F32) * (oy == (y + 4 - d) % 4).astype(F32)
            v2[...] = total.astype(BF)
            x_copy = send(v2.at[1 - x_hi], vx, (dp, (1 - x_hi) * 8 + y * 2 + c))
    rcv2[me] = snd2[me]

    x_copy.wait_recv()
    w = (who // 8 == x_hi).astype(F32)
    cond = v2[x_hi].astype(F32) * w + vx[...].astype(F32) * (1.0 - w)
    cn = (cond * lax.rsqrt(jnp.mean(cond * cond, axis=1, keepdims=True) + EPS)).astype(BF)
    xc[0, ROWS:] = cn
    cn_copy = send(xc.at[0, pl.ds(ROWS, VT)], xc.at[1, pl.ds(ROWS, VT)], pair)
    zeros = jnp.zeros((KEYS - ROWS - VT, INNER), BF)
    kk[ROWS : ROWS + VT] = nn(cn, wk[...]).astype(BF)
    vv[ROWS : ROWS + VT] = nn(cn, wv[...]).astype(BF)
    kk[ROWS + VT :] = zeros
    vv[ROWS + VT :] = zeros

    real = lax.broadcasted_iota(jnp.int32, (2 * ROWS, KEYS), 1) < ROWS + VT
    for p in range(5):
        cols = slice(p * 128, (p + 1) * 128)
        o, dq, dk, dv = attend(q_v[:, cols], kk[:, cols], vv[:, cols], go_v[:, cols], real)
        ov[:, cols] = o
        dqv[:, cols] = dq
        dkv_v[:, cols] = dk[: ROWS + VT]
        dvv_v[:, cols] = dv[: ROWS + VT]

    cn_copy.wait_recv()
    both = xc[...].reshape(2 * (ROWS + VT), D)
    xnp = [nt(pt[i], both).astype(BF) for i in range(2)]
    pt[0, :, : 2 * (ROWS + VT)] = xnp[0]
    pt[1, :, : 2 * (ROWS + VT)] = xnp[1]

    for n, (a, b) in enumerate(CHUNKS):
        lanes = pl.ds(a * 256, (b - a) * 256)
        for d in range(1, NF):
            arrived(rcv2.at[(me + NF - d) % NF, :, lanes], ar2.at[n, d])
        for p in range(a, b):
            cols = slice(p * 128, (p + 1) * 128)
            vcols = slice(INNER + p * 128, INNER + (p + 1) * 128)
            o, dk = unpack(rcv2[:, :, p * 256 : p * 256 + 128])
            dq, dv = unpack(rcv2[:, :, p * 256 + 128 : p * 256 + 256])
            h_v[:, cols] = (ov[:, cols] + o).astype(BF)
            dq_b[:, cols] = (dqv[:, cols] + dq).astype(BF)
            dkv[0, :ROWS, cols] = (dkv_v[:ROWS, cols] + dk).astype(BF)
            dkv[0, :ROWS, vcols] = (dvv_v[:ROWS, cols] + dv).astype(BF)
    dkv[0, ROWS:, :INNER] = dkv_v[ROWS:].astype(BF)
    dkv[0, ROWS:, INNER:] = dvv_v[ROWS:].astype(BF)
    dkv_copy = send(dkv.at[0], dkv.at[1], pair)
    dkv_copy.wait_recv()

    deep = 2 * (ROWS + VT)
    rhs = dkv[...].reshape(deep, D)
    xs, ys = [], []
    for d in (1, 2, 3, 0):
        bx = pl.multiple_of(((x + d) % 4) * 160, 32)
        gx[d] = nn(pt[0, pl.ds(bx, 160), :deep], rhs[:, :INNER]).astype(BF)
        if d:
            xs.append(send(gx.at[d], rx.at[d - 1], at_x(d)))
        by = pl.multiple_of(((y + d) % 4) * 160, 32)
        gy[d] = nn(pt[1, pl.ds(by, 160), :deep], rhs[:, INNER:]).astype(BF)
        if d:
            ys.append(send(gy.at[d], ry.at[d - 1], at_y(d)))

    block_v[...] = (lat_v[...].astype(F32) + nn(h_v[...], wo[...])).astype(BF)
    block_out = pltpu.make_async_copy(block_v, block_h, load_sem.at[7])
    block_out.start()
    mine = dkv[0, :ROWS]
    dn = nt(dq_b[...], wq[...]) + nt(mine[:, :INNER], wk[...]) + nt(mine[:, INNER:], wv[...])
    norm = normed[...]
    xf = lat_v[...].astype(F32)
    factor = lax.rsqrt(jnp.mean(xf * xf, axis=1, keepdims=True) + EPS)
    back = ogr_v[...].astype(F32) + factor * (dn - norm * jnp.mean(dn * norm, axis=1, keepdims=True))
    back_v[...] = back.astype(BF)
    back_out = pltpu.make_async_copy(back_v, back_h, load_sem.at[8])
    back_out.start()

    pad = jnp.zeros((8, INNER), F32)

    def first_sum(g, r, copies, at):
        total = g[0].astype(F32)
        for d in range(1, 4):
            copies[d - 1].wait_recv()
            total = total + r[d - 1].astype(F32)
        m1[at] = total

    def second_send(at, position, s2, r2, peer):
        copies = []
        for d in range(1, 4):
            rows = pl.multiple_of(((position + d) % 4) * 40, 8)
            s2[d] = jnp.concatenate([m1[at, pl.ds(rows, 40), :], pad], axis=0).astype(BF)
            copies.append(send(s2.at[d], r2.at[d - 1], peer(d)))
        return copies

    def second_sum(at, position, r2, copies):
        total = m1[at, pl.ds(pl.multiple_of(position * 40, 8), 40), :]
        for d in range(1, 4):
            copies[d - 1].wait_recv()
            total = total + r2[d - 1].astype(F32)[:40]
        return total.astype(BF)

    first_sum(gx, rx, xs, 0)
    x2 = second_send(0, y, s2x, r2x, at_y)
    first_sum(gy, ry, ys, 1)
    y2 = second_send(1, x, s2y, r2y, at_x)

    slot = lax.broadcasted_iota(jnp.int32, (128, 1), 0)
    sz, sk = slot >> 4, slot & 7
    source = jnp.where(sk < 5, ((slot >> 3) & 1) * 40 + sz * 5 + sk, -1)
    place = (source == lax.broadcasted_iota(jnp.int32, (1, 80), 1)).astype(F32).astype(BF)
    tx = second_sum(0, y, r2x, x2)
    ty = second_sum(1, x, r2y, y2)
    s3[...] = nn(place[:, :40], tx).astype(BF).reshape(8, 16, INNER) + nn(place[:, 40:], ty).astype(BF).reshape(
        8, 16, INNER
    )
    zs = [send(s3.at[(z + d) % 8], r3.at[d - 1], at_z(d)) for d in range(1, 8)]
    total = s3[z].astype(F32)
    for d in range(1, 8):
        zs[d - 1].wait_recv()
        total = total + r3[d - 1].astype(F32)
    grad_o[:, :INNER] = total[:5]
    grad_o[:, INNER:] = total[8:13]

    block_out.wait()
    back_out.wait()
    for copy in started:
        copy.wait_send()


def shards(latents, out_grad, video, owner, w_query, w_key, w_value, w_out):
    hbm = pl.BlockSpec(memory_space=pl.ANY)
    span = ROWS + VT
    vm = pltpu.VMEM
    dma = pltpu.SemaphoreType.DMA
    half = ((ROWS, INNER), BF)
    scratch = [
        vm((ROWS, D), BF), vm((ROWS, D), BF),
        vm((D, INNER), BF), vm((D, INNER), BF), vm((D, INNER), BF), vm((INNER, D), BF),
        vm((ROWS, D), BF), vm((ROWS, D), BF),
        vm((ROWS, D), F32), vm((2, span, D), BF),
        vm(*half), vm((KEYS, INNER), BF), vm((KEYS, INNER), BF), vm(*half),
        vm((NF, 16, D), BF), vm((NF, 16, D), BF), vm((NF, 16, D), BF), vm((NF, 16, D), BF),
        vm((8, VT, D), BF), vm((8, VT, D), BF), vm((2, 4, VT, D), BF), vm((3, 2, VT, D), BF),
        vm((2, VT, D), BF), vm((VT, D), BF),
        vm((ROWS, INNER), F32), vm((ROWS, INNER), F32), vm((span, INNER), F32), vm((span, INNER), F32),
        vm(*half), vm(*half), vm((2, span, D), BF),
        vm((2, INNER, D), BF),
        vm((4, 160, INNER), BF), vm((4, 160, INNER), BF), vm((3, 160, INNER), BF), vm((3, 160, INNER), BF),
        vm((4, 48, INNER), BF), vm((4, 48, INNER), BF), vm((3, 48, INNER), BF), vm((3, 48, INNER), BF),
        vm((2, 160, INNER), F32), vm((8, 16, INNER), BF), vm((7, 16, INNER), BF),
        dma((9,)), dma((NC, NF)), dma((NC, NF)), dma((NC, NF)), dma((NC, NF)), dma((32,)), dma((32,)),
    ]
    block, back, grads = pl.pallas_call(
        kernel,
        out_shape=(
            jax.ShapeDtypeStruct((ROWS, D), BF),
            jax.ShapeDtypeStruct((ROWS, D), BF),
            jax.ShapeDtypeStruct((5, D), F32),
        ),
        in_specs=[hbm, hbm, hbm, pl.BlockSpec(memory_space=pltpu.SMEM)] + [hbm] * 4,
        out_specs=(hbm, hbm, pl.BlockSpec(memory_space=pltpu.VMEM)),
        scratch_shapes=scratch,
        compiler_params=pltpu.CompilerParams(
            collective_id=0, has_side_effects=True, vmem_limit_bytes=48 * 1024 * 1024
        ),
    )(
        latents.reshape(ROWS, D),
        out_grad.reshape(ROWS, D),
        video.reshape(8, 2, VT, D),
        owner,
        w_query,
        w_key,
        w_value,
        w_out,
    )
    return block.reshape(latents.shape), back.reshape(latents.shape), grads


def solution(mesh):
    tokens = P("dp", "frame", None, None, None)
    return jax.shard_map(
        shards,
        mesh=mesh,
        in_specs=(tokens, tokens, tokens, P("dp"), P(), P(), P(), P()),
        out_specs=(tokens, tokens, P(("dp", "frame"), None)),
        check_vma=False,
    )
```

```python
import jax
import jax.numpy as jnp
from jax import lax
from jax.experimental import pallas as pl
from jax.experimental.pallas import tpu as pltpu
from jax.sharding import PartitionSpec as P

MESH = pl.DeviceIdType.MESH
BF = jnp.bfloat16
F32 = jnp.float32
D, INNER, HD = 1280, 640, 64
ROWS, VT, NF = 128, 32, 16
KEYS = 256
EPS = 1e-6
CHUNKS = ((0, 3), (3, 5))
TURNS = (8, 7, 9, 6, 10, 5, 11, 4, 12, 3, 13, 2, 14, 1, 15)
SLOTS = (4, 3, 5, 2, 6, 1, 7, 0)
ORDER = (2, 1, 3)
FAR = (4, 3, 5, 2, 6, 1, 7)


def nn(a, b):
    return jnp.dot(a, b, preferred_element_type=F32)


def nt(a, b):
    return lax.dot_general(a, b, (((1,), (1,)), ((), ())), preferred_element_type=F32)


def tn(a, b):
    return lax.dot_general(a, b, (((0,), (0,)), ((), ())), preferred_element_type=F32)


def attend(q, k, v, go, mask):
    lane = lax.broadcasted_iota(jnp.int32, (1, 128), 1)
    first = (lane < HD).astype(F32).astype(BF)
    second = (lane >= HD).astype(F32).astype(BF)
    qm = jnp.concatenate([q * first, q * second], axis=0)
    gm = jnp.concatenate([go * first, go * second], axis=0)
    km = jnp.concatenate([k * first, k * second], axis=0)
    vm = jnp.concatenate([v * first, v * second], axis=0)
    e = jnp.where(mask, jnp.exp(nt(qm, k) * 0.125), 0.0)
    dp = nt(gm, v)
    r = 1.0 / jnp.sum(e, axis=1, keepdims=True)
    eb = e.astype(BF)
    o = nn(jnp.concatenate([eb[:ROWS], eb[ROWS:]], axis=1), vm)
    o = o * jnp.where(lane < HD, r[:ROWS], r[ROWS:])
    delta = jnp.sum(gm.astype(F32) * jnp.concatenate([o, o], axis=0), axis=1, keepdims=True)
    p = e * r
    ds = (p * (dp - delta)).astype(BF)
    dq = nn(jnp.concatenate([ds[:ROWS], ds[ROWS:]], axis=1), km) * 0.125
    dk = tn(ds, qm) * 0.125
    dv = tn(p.astype(BF), gm)
    return o, dq, dk, dv


def fold(left, right):
    n, m = left.shape[1], right.shape[1]
    if m < n:
        right = jnp.concatenate([right, jnp.zeros((ROWS, n - m), F32)], axis=1)
    return jnp.concatenate([left.reshape(NF, 8, n), right.reshape(NF, 8, n)], axis=1).astype(BF)


def unfold(block, m):
    wide = block.astype(F32)
    n = wide.shape[2]
    return jnp.concatenate([wide[:, :8].reshape(ROWS, n), wide[:, 8:, :m].reshape(ROWS, m)], axis=1)


def kernel(
    lat, ogr, vid, own, wq_h, wk_h, wv_h, wo_h,
    block_h, back_h, grad_o,
    lat_v, ogr_v, wq, wk, wv, wo, block_v, back_v, grad_v,
    normed, xt, q_v, kk, vv, go_v, sx, sg, ax, ag, so, sd, ro, rd,
    va, vb, vs, vr, ov, dqv, dqt, dkv,
    pt, xp, gx, gy, rx, ry, s2x, s2y, r2x, r2y, m1, s3, r3,
    load_sem, as1, ar1, as2, ar2, ms, mr,
):
    dp = lax.axis_index("dp")
    me = lax.axis_index("frame")
    z, x_lo = dp // 2, dp % 2
    x_hi, y, c = me // 8, (me // 2) % 4, me % 2
    x = x_hi * 2 + x_lo

    def at_x(d):
        to = (x + d) % 4
        return (z * 2 + to % 2, (to // 2) * 8 + y * 2 + c)

    def at_y(d):
        return (dp, x_hi * 8 + ((y + d) % 4) * 2 + c)

    def at_z(d):
        return (((z + d) % 8) * 2 + x_lo, me)

    def at_f(d):
        return (dp, (me + d) % NF)

    pair = (dp, me + 1 - 2 * c)

    loads = [
        pltpu.make_async_copy(src, dst, load_sem.at[i])
        for i, (src, dst) in enumerate(
            [(lat, lat_v), (ogr, ogr_v), (wo_h, wo), (wq_h, wq), (wk_h, wk), (wv_h, wv), (vid.at[:, c], va)]
        )
    ]
    loads[0].start()

    barrier = pltpu.get_barrier_semaphore()
    peers = [at_f(d) for d in range(1, NF)] + [at_x(1), at_x(3)] + [at_z(d) for d in range(1, 8)]
    for peer in peers:
        pl.semaphore_signal(barrier, inc=1, device_id=peer, device_id_type=MESH)
    for copy in loads[1:]:
        copy.start()

    count = [0]
    started = []

    def send(src, dst, peer, ss=None, rs=None):
        if ss is None:
            ss, rs = ms.at[count[0]], mr.at[count[0]]
            count[0] += 1
        copy = pltpu.make_async_remote_copy(
            src_ref=src, dst_ref=dst, send_sem=ss, recv_sem=rs, device_id=peer, device_id_type=MESH
        )
        copy.start()
        started.append(copy)
        return copy

    def scatter(src, dst, ss, rs):
        for d in TURNS:
            send(src.at[(me + d) % NF], dst.at[me], at_f(d), ss.at[d], rs.at[d])

    def gathered(src, dst, rs):
        dst[me] = src[me]
        for d in TURNS:
            slot = dst.at[(me + NF - d) % NF]
            pltpu.make_async_remote_copy(
                src_ref=slot, dst_ref=slot, send_sem=rs.at[d], recv_sem=rs.at[d], device_id=pair, device_id_type=MESH
            ).wait_recv()

    def to_pair(ref, row, rows, cols=None):
        if cols is None:
            return send(ref.at[pl.ds(row, rows)], ref.at[pl.ds(row + rows, rows)], pair)
        return send(ref.at[:, pl.ds(row, rows), cols], ref.at[:, pl.ds(row + rows, rows), cols], pair)

    loads[0].wait()
    xf = lat_v[...].astype(F32)
    factor = lax.rsqrt(jnp.mean(xf * xf, axis=1, keepdims=True) + EPS)
    norm = xf * factor
    normed[...] = norm
    xt[:ROWS] = norm.astype(BF)
    sx[...] = fold(norm[:, :INNER], norm[:, INNER:])
    loads[1].wait()
    loads[2].wait()
    gf = nt(ogr_v[...], wo[...])
    sg[...] = fold(gf[:, :384], gf[:, 384:])
    go_v[...] = gf.astype(BF)

    pl.semaphore_wait(barrier, len(peers))
    core_copies = [send(vid.at[(me // 2 + d) % 8, 1 - c], vb.at[d], pair) for d in SLOTS]
    scatter(sx, ax, as1.at[0], ar1.at[0])
    scatter(sg, ag, as1.at[1], ar1.at[1])
    xn_copy = to_pair(xt, 0, ROWS)

    for copy in loads[3:6]:
        copy.wait()
    xn = xt[:ROWS]
    q_v[...] = nn(xn, wq[...]).astype(BF)
    kk[:ROWS] = nn(xn, wk[...]).astype(BF)
    vv[:ROWS] = nn(xn, wv[...]).astype(BF)

    who = own[0]
    loads[6].wait()
    w = (who % 2 == c).astype(F32)
    video_copies = {}
    for copy, d in zip(core_copies, SLOTS):
        copy.wait_recv()
        to = (me // 2 + d) % 8
        vs[d] = (va[to].astype(F32) * w + vb[d].astype(F32) * (1.0 - w)).astype(BF)
        if d:
            video_copies[d] = send(vs.at[d], vr.at[d], (dp, to * 2 + c))

    new = lax.broadcasted_iota(jnp.int32, (INNER, 1), 0)
    u = (new * 52429) >> 18
    k5 = new - 5 * u
    uz, lo, hi = u & 7, (u >> 3) & 3, u >> 5
    column = lax.broadcasted_iota(jnp.int32, (1, D), 1)

    def one_hot(ux, uy):
        old = ((((uz * 2 + (ux & 1)) * 2 + (ux >> 1)) * 4 + uy) * 2 + c) * 5 + k5
        return (old == column).astype(F32).astype(BF)

    pt[0] = one_hot(hi, lo)
    pt[1] = one_hot(lo, hi)

    def permute(first, last):
        rows = xt[first:last]
        for i in range(2):
            xp[i, :, first:last] = nt(pt[i], rows).astype(BF)

    gathered(sx, ax, ar1.at[0])
    xa = unfold(ax[...], INNER).astype(BF)
    xt[2 * ROWS : 3 * ROWS] = xa
    xa_copy = to_pair(xt, 2 * ROWS, ROWS)
    qa = nn(xa, wq[...]).astype(BF)
    ka = nn(xa, wk[...]).astype(BF)
    va_t = nn(xa, wv[...]).astype(BF)
    same = (
        (lax.broadcasted_iota(jnp.int32, (2 * ROWS, ROWS), 0) - lax.broadcasted_iota(jnp.int32, (2 * ROWS, ROWS), 1)) & 7
    ) == 0
    gathered(sg, ag, ar1.at[1])
    ga = unfold(ag[...], 256).astype(BF)
    outs = []
    for p in range(5):
        cols = slice(p * 128, (p + 1) * 128)
        o, dq, dk, dv = attend(qa[:, cols], ka[:, cols], va_t[:, cols], ga[:, cols], same)
        outs.append(o)
        dqt[:, cols] = dq.astype(BF)
        dkv[0, 2 * ROWS : 3 * ROWS, cols] = dk.astype(BF)
        dkv[1, 2 * ROWS : 3 * ROWS, cols] = dv.astype(BF)
    so[...] = fold(jnp.concatenate(outs[:3], axis=1), jnp.concatenate(outs[3:], axis=1))
    dn = nt(dqt[...], wq[...]) + nt(dkv[0, 2 * ROWS : 3 * ROWS], wk[...]) + nt(dkv[1, 2 * ROWS : 3 * ROWS], wv[...])
    sd[...] = fold(dn[:, :INNER], dn[:, INNER:])
    scatter(sd, rd, as2.at[0], ar2.at[0])
    scatter(so, ro, as2.at[1], ar2.at[1])
    dt_copy = to_pair(dkv, 2 * ROWS, ROWS, pl.ds(0, INNER))

    xn_copy.wait_recv()
    permute(0, 2 * ROWS)
    xa_copy.wait_recv()
    permute(2 * ROWS, 4 * ROWS)

    cond = vs[0].astype(F32) * (who // 2 == me // 2).astype(F32)
    for d in SLOTS:
        if d:
            video_copies[d].wait_recv()
            cond = cond + vr[d].astype(F32) * (who // 2 == (me // 2 + 8 - d) % 8).astype(F32)
    cn = (cond * lax.rsqrt(jnp.mean(cond * cond, axis=1, keepdims=True) + EPS)).astype(BF)
    xt[4 * ROWS : 4 * ROWS + VT] = cn
    cn_copy = to_pair(xt, 4 * ROWS, VT)
    zeros = jnp.zeros((KEYS - ROWS - VT, INNER), BF)
    kk[ROWS : ROWS + VT] = nn(cn, wk[...]).astype(BF)
    vv[ROWS : ROWS + VT] = nn(cn, wv[...]).astype(BF)
    kk[ROWS + VT :] = zeros
    vv[ROWS + VT :] = zeros
    real = lax.broadcasted_iota(jnp.int32, (2 * ROWS, KEYS), 1) < ROWS + VT
    late = []
    for a, b in CHUNKS:
        for p in range(a, b):
            cols = slice(p * 128, (p + 1) * 128)
            o, dq, dk, dv = attend(q_v[:, cols], kk[:, cols], vv[:, cols], go_v[:, cols], real)
            ov[:, cols] = o
            dqv[:, cols] = dq.astype(BF)
            for i, t in enumerate((dk.astype(BF), dv.astype(BF))):
                dkv[i, :ROWS, cols] = t[:ROWS]
                dkv[i, 4 * ROWS : 4 * ROWS + VT, cols] = t[ROWS : ROWS + VT]
        span = pl.ds(a * 128, (b - a) * 128)
        late.append((to_pair(dkv, 0, ROWS, span), to_pair(dkv, 4 * ROWS, VT, span)))
    cn_copy.wait_recv()
    permute(4 * ROWS, 4 * ROWS + 2 * VT)
    dt_copy.wait_recv()

    xs, ys = [], []
    for n, (a, b) in enumerate(CHUNKS):
        cols = slice(a * 128, b * 128)
        span = pl.ds(a * 128, (b - a) * 128)
        for copy in late[n]:
            copy.wait_recv()
        for d in (2, 1, 3, 0):
            bx = pl.multiple_of(((x + d) % 4) * 160, 32)
            gx[d, :, cols] = nn(xp[0, pl.ds(bx, 160), :], dkv[0, :, cols]).astype(BF)
            if d:
                xs.append(send(gx.at[d, :, span], rx.at[d - 1, :, span], at_x(d)))
            by = pl.multiple_of(((y + d) % 4) * 160, 32)
            gy[d, :, cols] = nn(xp[1, pl.ds(by, 160), :], dkv[1, :, cols]).astype(BF)
            if d:
                ys.append(send(gy.at[d, :, span], ry.at[d - 1, :, span], at_y(d)))

    gathered(so, ro, ar2.at[1])
    hidden = (ov[...] + unfold(ro[...], 256)).astype(BF)
    block_v[...] = (lat_v[...].astype(F32) + nn(hidden, wo[...])).astype(BF)
    block_out = pltpu.make_async_copy(block_v, block_h, load_sem.at[7])
    block_out.start()
    gathered(sd, rd, ar2.at[0])
    dn = nt(dqv[...], wq[...]) + nt(dkv[0, :ROWS], wk[...]) + nt(dkv[1, :ROWS], wv[...]) + unfold(rd[...], INNER)
    norm = normed[...]
    xf = lat_v[...].astype(F32)
    factor = lax.rsqrt(jnp.mean(xf * xf, axis=1, keepdims=True) + EPS)
    back = ogr_v[...].astype(F32) + factor * (dn - norm * jnp.mean(dn * norm, axis=1, keepdims=True))
    back_v[...] = back.astype(BF)
    back_out = pltpu.make_async_copy(back_v, back_h, load_sem.at[8])
    back_out.start()

    def first_sum(at, g, r, copies, cols):
        total = g[0, :, cols].astype(F32)
        for i, copy in enumerate(copies):
            copy.wait_recv()
            total = total + r[ORDER[i] - 1, :, cols].astype(F32)
        m1[at, :, cols] = total

    def second_send(at, position, s2, r2, peer, cols, span):
        pad = jnp.zeros((8, cols.stop - cols.start), F32)
        copies = []
        for d in ORDER:
            rows = pl.multiple_of(((position + d) % 4) * 40, 8)
            s2[d, :, cols] = jnp.concatenate([m1[at, pl.ds(rows, 40), cols], pad], axis=0).astype(BF)
            copies.append(send(s2.at[d, :, span], r2.at[d - 1, :, span], peer(d)))
        return copies

    def second_sum(at, position, r2, copies, cols):
        total = m1[at, pl.ds(pl.multiple_of(position * 40, 8), 40), cols]
        for i, copy in enumerate(copies):
            copy.wait_recv()
            total = total + r2[ORDER[i] - 1, :, cols].astype(F32)[:40]
        return total.astype(BF)

    x2, y2, zs = [], [], []
    for n, (a, b) in enumerate(CHUNKS):
        cols, span = slice(a * 128, b * 128), pl.ds(a * 128, (b - a) * 128)
        first_sum(0, gx, rx, xs[3 * n : 3 * n + 3], cols)
        x2.append(second_send(0, y, s2x, r2x, at_y, cols, span))
        first_sum(1, gy, ry, ys[3 * n : 3 * n + 3], cols)
        y2.append(second_send(1, x, s2y, r2y, at_x, cols, span))

    slot = lax.broadcasted_iota(jnp.int32, (128, 1), 0)
    sz, sk = slot >> 4, slot & 7
    source = jnp.where(sk < 5, ((slot >> 3) & 1) * 40 + sz * 5 + sk, -1)
    place = (source == lax.broadcasted_iota(jnp.int32, (1, 80), 1)).astype(F32).astype(BF)
    for n, (a, b) in enumerate(CHUNKS):
        cols, span = slice(a * 128, b * 128), pl.ds(a * 128, (b - a) * 128)
        tx = second_sum(0, y, r2x, x2[n], cols)
        ty = second_sum(1, x, r2y, y2[n], cols)
        spread = nn(place[:, :40], tx) + nn(place[:, 40:], ty)
        s3[:, :, cols] = spread.astype(BF).reshape(8, 16, cols.stop - cols.start)
        zs.append([send(s3.at[(z + d) % 8, :, span], r3.at[d - 1, :, span], at_z(d)) for d in FAR])
    for n, (a, b) in enumerate(CHUNKS):
        cols = slice(a * 128, b * 128)
        total = s3[z, :, cols].astype(F32)
        for d, copy in zip(FAR, zs[n]):
            copy.wait_recv()
            total = total + r3[d - 1, :, cols].astype(F32)
        grad_v[:, cols] = total[:5]
        grad_v[:, INNER + a * 128 : INNER + b * 128] = total[8:13]

    grad_out = pltpu.make_async_copy(grad_v, grad_o, load_sem.at[9])
    grad_out.start()
    grad_out.wait()
    block_out.wait()
    back_out.wait()
    for copy in started:
        copy.wait_send()


def finish(a, b, c, a_out, b_out, c_out, a_v, b_v, c_v, sem):
    trio = ((a, a_v, a_out), (b, b_v, b_out), (c, c_v, c_out))
    reads = [pltpu.make_async_copy(t[0], t[1], sem.at[0, i]) for i, t in enumerate(trio)]
    writes = [pltpu.make_async_copy(t[1], t[2], sem.at[1, i]) for i, t in enumerate(trio)]
    for copy in reads:
        copy.start()
    for read, write in zip(reads, writes):
        read.wait()
        write.start()
    for copy in writes:
        copy.wait()


def shards(latents, out_grad, video, owner, w_query, w_key, w_value, w_out):
    hbm = pl.BlockSpec(memory_space=pltpu.HBM)
    deep = 4 * ROWS + 2 * VT
    vm = pltpu.VMEM
    dma = pltpu.SemaphoreType.DMA
    half = ((ROWS, INNER), BF)
    scratch = [
        vm((ROWS, D), BF), vm((ROWS, D), BF),
        vm((D, INNER), BF), vm((D, INNER), BF), vm((D, INNER), BF), vm((INNER, D), BF),
        vm((ROWS, D), BF), vm((ROWS, D), BF), vm((5, D), F32),
        vm((ROWS, D), F32), vm((deep, D), BF),
        vm(*half), vm((KEYS, INNER), BF), vm((KEYS, INNER), BF), vm(*half),
        vm((NF, 16, INNER), BF), vm((NF, 16, 384), BF), vm((NF, 16, INNER), BF), vm((NF, 16, 384), BF),
        vm((NF, 16, 384), BF), vm((NF, 16, INNER), BF), vm((NF, 16, 384), BF), vm((NF, 16, INNER), BF),
        vm((8, VT, D), BF), vm((8, VT, D), BF), vm((8, VT, D), BF), vm((8, VT, D), BF),
        vm((ROWS, INNER), F32), vm(*half), vm(*half), vm((2, deep, INNER), BF),
        vm((2, INNER, D), BF), vm((2, INNER, deep), BF),
        vm((4, 160, INNER), BF), vm((4, 160, INNER), BF), vm((3, 160, INNER), BF), vm((3, 160, INNER), BF),
        vm((4, 48, INNER), BF), vm((4, 48, INNER), BF), vm((3, 48, INNER), BF), vm((3, 48, INNER), BF),
        vm((2, 160, INNER), F32), vm((8, 16, INNER), BF), vm((7, 16, INNER), BF),
        dma((10,)), dma((2, NF)), dma((2, NF)), dma((2, NF)), dma((2, NF)), dma((80,)), dma((80,)),
    ]
    block, back, grads = pl.pallas_call(
        kernel,
        out_shape=(
            jax.ShapeDtypeStruct((ROWS, D), BF),
            jax.ShapeDtypeStruct((ROWS, D), BF),
            jax.ShapeDtypeStruct((5, D), F32),
        ),
        in_specs=[hbm, hbm, hbm, pl.BlockSpec(memory_space=pltpu.SMEM)] + [hbm] * 4,
        out_specs=(hbm, hbm, hbm),
        scratch_shapes=scratch,
        compiler_params=pltpu.CompilerParams(
            collective_id=0, has_side_effects=True, vmem_limit_bytes=62 * 1024 * 1024
        ),
    )(
        latents.reshape(ROWS, D),
        out_grad.reshape(ROWS, D),
        video.reshape(8, 2, VT, D),
        owner,
        w_query,
        w_key,
        w_value,
        w_out,
    )
    block, back, grads = pl.pallas_call(
        finish,
        out_shape=(
            jax.ShapeDtypeStruct((ROWS, D), BF),
            jax.ShapeDtypeStruct((ROWS, D), BF),
            jax.ShapeDtypeStruct((5, D), F32),
        ),
        in_specs=[hbm] * 3,
        out_specs=[hbm] * 3,
        scratch_shapes=[vm((ROWS, D), BF), vm((ROWS, D), BF), vm((5, D), F32), dma((2, 3))],
        compiler_params=pltpu.CompilerParams(vmem_limit_bytes=62 * 1024 * 1024),
    )(block, back, grads)
    return block.reshape(latents.shape), back.reshape(latents.shape), grads


def solution(mesh):
    tokens = P("dp", "frame", None, None, None)
    return jax.shard_map(
        shards,
        mesh=mesh,
        in_specs=(tokens, tokens, tokens, P("dp"), P(), P(), P(), P()),
        out_specs=(tokens, tokens, P(("dp", "frame"), None)),
        check_vma=False,
    )
```

```python
import jax
import jax.numpy as jnp
from jax import lax
from jax.experimental import pallas as pl
from jax.experimental.pallas import tpu as pltpu
from jax.sharding import PartitionSpec as P

MESH = pl.DeviceIdType.MESH
BF = jnp.bfloat16
F32 = jnp.float32
D, INNER, HD = 1280, 640, 64
ROWS, VT, NF = 128, 32, 16
KEYS = 256
EPS = 1e-6
CHUNKS = ((0, 2), (2, 5))
TURNS = (12, 4, 13, 5, 10, 2, 14, 6, 11, 3, 15, 7, 8, 9, 1)
SLOTS = (6, 2, 5, 1, 7, 3, 4, 0)
ORDER = (2, 1, 3)
FAR = (4, 3, 5, 2, 6, 1, 7)


def nn(a, b):
    return jnp.dot(a, b, preferred_element_type=F32)


def nt(a, b):
    return lax.dot_general(a, b, (((1,), (1,)), ((), ())), preferred_element_type=F32)


def tn(a, b):
    return lax.dot_general(a, b, (((0,), (0,)), ((), ())), preferred_element_type=F32)


def attend(q, k, v, go, mask):
    lane = lax.broadcasted_iota(jnp.int32, (1, 128), 1)
    first = (lane < HD).astype(F32).astype(BF)
    second = (lane >= HD).astype(F32).astype(BF)
    qm = jnp.concatenate([q * first, q * second], axis=0)
    gm = jnp.concatenate([go * first, go * second], axis=0)
    km = jnp.concatenate([k * first, k * second], axis=0)
    vm = jnp.concatenate([v * first, v * second], axis=0)
    e = jnp.where(mask, jnp.exp(nt(qm, k) * 0.125), 0.0)
    dp = nt(gm, v)
    r = 1.0 / jnp.sum(e, axis=1, keepdims=True)
    eb = e.astype(BF)
    o = nn(jnp.concatenate([eb[:ROWS], eb[ROWS:]], axis=1), vm)
    o = o * jnp.where(lane < HD, r[:ROWS], r[ROWS:])
    delta = jnp.sum(gm.astype(F32) * jnp.concatenate([o, o], axis=0), axis=1, keepdims=True)
    p = e * r
    ds = (p * (dp - delta)).astype(BF)
    dq = nn(jnp.concatenate([ds[:ROWS], ds[ROWS:]], axis=1), km) * 0.125
    dk = tn(ds, qm) * 0.125
    dv = tn(p.astype(BF), gm)
    return o, dq, dk, dv


def fold(left, right):
    n, m = left.shape[1], right.shape[1]
    if m < n:
        right = jnp.concatenate([right, jnp.zeros((ROWS, n - m), F32)], axis=1)
    return jnp.concatenate([left.reshape(NF, 8, n), right.reshape(NF, 8, n)], axis=1).astype(BF)


def unfold(block, m):
    wide = block.astype(F32)
    n = wide.shape[2]
    return jnp.concatenate([wide[:, :8].reshape(ROWS, n), wide[:, 8:, :m].reshape(ROWS, m)], axis=1)


def kernel(
    lat, ogr, vid, own, wq_h, wk_h, wv_h, wo_h,
    block_h, back_h, grad_o,
    own_s, lat_v, ogr_v, wq, wk, wv, wo, block_v, back_v, grad_v,
    normed, xt, q_v, kk, vv, go_v, sx, ax, so, ro,
    va, vb, vs, vr, ov, dqv, dqt, dkv,
    pt, xp, gx, gy, rx, ry, s2x, s2y, r2x, r2y, m1, s3, r3,
    load_sem, as1, ar1, as2, ar2, ms, mr,
):
    dp = lax.axis_index("dp")
    me = lax.axis_index("frame")
    z, x_lo = dp // 2, dp % 2
    x_hi, y, c = me // 8, (me // 2) % 4, me % 2
    x = x_hi * 2 + x_lo

    def at_x(d):
        to = (x + d) % 4
        return (z * 2 + to % 2, (to // 2) * 8 + y * 2 + c)

    def at_y(d):
        return (dp, x_hi * 8 + ((y + d) % 4) * 2 + c)

    def at_z(d):
        return (((z + d) % 8) * 2 + x_lo, me)

    def to_f(d):
        return ((x_hi + d // 8) % 2) * 8 + ((y + (d // 2) % 4) % 4) * 2 + (c + d) % 2

    def from_f(d):
        return ((x_hi + d // 8) % 2) * 8 + ((y + 4 - (d // 2) % 4) % 4) * 2 + (c + d) % 2

    def at_f(d):
        return (dp, to_f(d))

    pair = (dp, me + 1 - 2 * c)

    loads = [
        pltpu.make_async_copy(src, dst, load_sem.at[i])
        for i, (src, dst) in enumerate(
            [(lat, lat_v), (ogr, ogr_v), (wo_h, wo), (wq_h, wq), (wk_h, wk), (wv_h, wv), (vid, va)]
        )
    ]
    loads[0].start()

    barrier = pltpu.get_barrier_semaphore()
    peers = [at_z(d) for d in FAR] + [at_x(1), at_x(3)] + [at_f(d) for d in TURNS]
    for peer in peers:
        pl.semaphore_signal(barrier, inc=1, device_id=peer, device_id_type=MESH)
    for copy in loads[1:]:
        copy.start()
    owner_copy = pltpu.make_async_copy(own, own_s, load_sem.at[10])
    owner_copy.start()

    count = [0]
    started = []

    def send(src, dst, peer, ss=None, rs=None):
        if ss is None:
            ss, rs = ms.at[count[0]], mr.at[count[0]]
            count[0] += 1
        copy = pltpu.make_async_remote_copy(
            src_ref=src, dst_ref=dst, send_sem=ss, recv_sem=rs, device_id=peer, device_id_type=MESH
        )
        copy.start()
        started.append(copy)
        return copy

    def scatter(src, dst, ss, rs):
        for d in TURNS:
            send(src.at[to_f(d)], dst.at[me], at_f(d), ss.at[d], rs.at[d])

    def gathered(src, dst, rs):
        dst[me] = src[me]
        for d in TURNS:
            slot = dst.at[from_f(d)]
            pltpu.make_async_remote_copy(
                src_ref=slot, dst_ref=slot, send_sem=rs.at[d], recv_sem=rs.at[d], device_id=pair, device_id_type=MESH
            ).wait_recv()

    def to_pair(ref, row, rows, cols=None):
        if cols is None:
            return send(ref.at[pl.ds(row, rows)], ref.at[pl.ds(row + rows, rows)], pair)
        return send(ref.at[:, pl.ds(row, rows), cols], ref.at[:, pl.ds(row + rows, rows), cols], pair)

    loads[0].wait()
    xf = lat_v[...].astype(F32)
    factor = lax.rsqrt(jnp.mean(xf * xf, axis=1, keepdims=True) + EPS)
    norm = xf * factor
    normed[...] = norm
    xt[:ROWS] = norm.astype(BF)
    sx[:, :, :INNER] = fold(norm[:, :INNER], norm[:, INNER:])
    loads[1].wait()
    loads[2].wait()
    gf = nt(ogr_v[...], wo[...])
    sx[:, :, INNER:] = fold(gf[:, :384], gf[:, 384:])
    go_v[...] = gf.astype(BF)

    pl.semaphore_wait(barrier, len(peers))
    loads[6].wait()
    core_copy = send(va.at[:, 1 - c], vb, pair)
    scatter(sx, ax, as1.at[0], ar1.at[0])
    xn_copy = to_pair(xt, 0, ROWS)

    kk[ROWS + VT :] = jnp.zeros((KEYS - ROWS - VT, INNER), BF)
    vv[ROWS + VT :] = jnp.zeros((KEYS - ROWS - VT, INNER), BF)
    owner_copy.wait()
    who = own_s[0]
    w = (who % 2 == c).astype(F32)
    video_copies = {}
    core_copy.wait_recv()
    for d in SLOTS:
        to = ((x_hi + d // 4) % 2) * 4 + (y + d) % 4
        vs[d] = (va[to, c].astype(F32) * w + vb[to].astype(F32) * (1.0 - w)).astype(BF)
        if d:
            video_copies[d] = send(vs.at[d], vr.at[d], (dp, to * 2 + c))

    for copy in loads[3:6]:
        copy.wait()
    xn = xt[:ROWS]
    q_v[...] = nn(xn, wq[...]).astype(BF)
    kk[:ROWS] = nn(xn, wk[...]).astype(BF)
    vv[:ROWS] = nn(xn, wv[...]).astype(BF)

    new = lax.broadcasted_iota(jnp.int32, (INNER, 1), 0)
    u = (new * 52429) >> 18
    k5 = new - 5 * u
    uz, lo, hi = u & 7, (u >> 3) & 3, u >> 5
    column = lax.broadcasted_iota(jnp.int32, (1, D), 1)

    def one_hot(ux, uy):
        old = ((((uz * 2 + (ux & 1)) * 2 + (ux >> 1)) * 4 + uy) * 2 + c) * 5 + k5
        return (old == column).astype(F32).astype(BF)

    pt[0] = one_hot(hi, lo)
    pt[1] = one_hot(lo, hi)

    def permute(first, last):
        rows = xt[first:last]
        for i in range(2):
            xp[i, :, first:last] = nt(pt[i], rows).astype(BF)

    xn_copy.wait_recv()
    permute(0, 2 * ROWS)

    gathered(sx, ax, ar1.at[0])
    xa = unfold(ax[:, :, :INNER], INNER).astype(BF)
    xt[2 * ROWS : 3 * ROWS] = xa
    xa_copy = to_pair(xt, 2 * ROWS, ROWS)
    qa = nn(xa, wq[...]).astype(BF)
    ka = nn(xa, wk[...]).astype(BF)
    va_t = nn(xa, wv[...]).astype(BF)
    same = (
        (lax.broadcasted_iota(jnp.int32, (2 * ROWS, ROWS), 0) - lax.broadcasted_iota(jnp.int32, (2 * ROWS, ROWS), 1)) & 7
    ) == 0
    ga = unfold(ax[:, :, INNER:], 256).astype(BF)
    outs = []
    for p in range(5):
        cols = slice(p * 128, (p + 1) * 128)
        o, dq, dk, dv = attend(qa[:, cols], ka[:, cols], va_t[:, cols], ga[:, cols], same)
        outs.append(o)
        dqt[:, cols] = dq.astype(BF)
        dkv[0, 2 * ROWS : 3 * ROWS, cols] = dk.astype(BF)
        dkv[1, 2 * ROWS : 3 * ROWS, cols] = dv.astype(BF)
    so[:, :, INNER:] = fold(jnp.concatenate(outs[:3], axis=1), jnp.concatenate(outs[3:], axis=1))
    dn = nt(dqt[...], wq[...]) + nt(dkv[0, 2 * ROWS : 3 * ROWS], wk[...]) + nt(dkv[1, 2 * ROWS : 3 * ROWS], wv[...])
    so[:, :, :INNER] = fold(dn[:, :INNER], dn[:, INNER:])
    dt_copy = to_pair(dkv, 2 * ROWS, ROWS, pl.ds(0, INNER))

    scatter(so, ro, as2.at[0], ar2.at[0])
    xa_copy.wait_recv()
    permute(2 * ROWS, 4 * ROWS)

    cond = vs[0].astype(F32) * (who // 2 == me // 2).astype(F32)
    for d in SLOTS:
        if d:
            video_copies[d].wait_recv()
            cond = cond + vr[d].astype(F32) * (who // 2 == ((x_hi + d // 4) % 2) * 4 + (y + 8 - d) % 4).astype(F32)
    cn = (cond * lax.rsqrt(jnp.mean(cond * cond, axis=1, keepdims=True) + EPS)).astype(BF)
    xt[4 * ROWS : 4 * ROWS + VT] = cn
    cn_copy = to_pair(xt, 4 * ROWS, VT)
    real = lax.broadcasted_iota(jnp.int32, (2 * ROWS, KEYS), 1) < ROWS + VT
    xs, ys = [], []
    for n, (a, b) in enumerate(CHUNKS):
        cols, span = slice(a * 128, b * 128), pl.ds(a * 128, (b - a) * 128)
        kk[ROWS : ROWS + VT, cols] = nn(cn, wk[:, cols]).astype(BF)
        vv[ROWS : ROWS + VT, cols] = nn(cn, wv[:, cols]).astype(BF)
        for p in range(a, b):
            part = slice(p * 128, (p + 1) * 128)
            o, dq, dk, dv = attend(q_v[:, part], kk[:, part], vv[:, part], go_v[:, part], real)
            ov[:, part] = o
            dqv[:, part] = dq.astype(BF)
            for i, t in enumerate((dk.astype(BF), dv.astype(BF))):
                dkv[i, :ROWS, part] = t[:ROWS]
                dkv[i, 4 * ROWS : 4 * ROWS + VT, part] = t[ROWS : ROWS + VT]
        late = (to_pair(dkv, 0, ROWS, span), to_pair(dkv, 4 * ROWS, VT, span))
        if n == 0:
            cn_copy.wait_recv()
            permute(4 * ROWS, 4 * ROWS + 2 * VT)
            dt_copy.wait_recv()
        for copy in late:
            copy.wait_recv()
        for d in (2, 1, 3, 0):
            bx = pl.multiple_of(((x + d) % 4) * 160, 32)
            gx[d, :, cols] = nn(xp[0, pl.ds(bx, 160), :], dkv[0, :, cols]).astype(BF)
            if d:
                xs.append(send(gx.at[d, :, span], rx.at[d - 1, :, span], at_x(d)))
            by = pl.multiple_of(((y + d) % 4) * 160, 32)
            gy[d, :, cols] = nn(xp[1, pl.ds(by, 160), :], dkv[1, :, cols]).astype(BF)
            if d:
                ys.append(send(gy.at[d, :, span], ry.at[d - 1, :, span], at_y(d)))

    gathered(so, ro, ar2.at[0])
    hidden = (ov[...] + unfold(ro[:, :, INNER:], 256)).astype(BF)
    block_v[...] = (lat_v[...].astype(F32) + nn(hidden, wo[...])).astype(BF)
    block_out = pltpu.make_async_copy(block_v, block_h, load_sem.at[7])
    block_out.start()
    dn = nt(dqv[...], wq[...]) + nt(dkv[0, :ROWS], wk[...]) + nt(dkv[1, :ROWS], wv[...]) + unfold(ro[:, :, :INNER], INNER)
    norm = normed[...]
    xf = lat_v[...].astype(F32)
    factor = lax.rsqrt(jnp.mean(xf * xf, axis=1, keepdims=True) + EPS)
    back = ogr_v[...].astype(F32) + factor * (dn - norm * jnp.mean(dn * norm, axis=1, keepdims=True))
    back_v[...] = back.astype(BF)
    back_out = pltpu.make_async_copy(back_v, back_h, load_sem.at[8])
    back_out.start()

    def first_sum(at, g, r, copies, cols):
        total = g[0, :, cols].astype(F32)
        for i, copy in enumerate(copies):
            copy.wait_recv()
            total = total + r[ORDER[i] - 1, :, cols].astype(F32)
        m1[at, :, cols] = total

    def second_send(at, position, s2, r2, peer, cols, span):
        pad = jnp.zeros((8, cols.stop - cols.start), F32)
        copies = []
        for d in ORDER:
            rows = pl.multiple_of(((position + d) % 4) * 40, 8)
            s2[d, :, cols] = jnp.concatenate([m1[at, pl.ds(rows, 40), cols], pad], axis=0).astype(BF)
            copies.append(send(s2.at[d, :, span], r2.at[d - 1, :, span], peer(d)))
        return copies

    def second_sum(at, position, r2, copies, cols):
        total = m1[at, pl.ds(pl.multiple_of(position * 40, 8), 40), cols]
        for i, copy in enumerate(copies):
            copy.wait_recv()
            total = total + r2[ORDER[i] - 1, :, cols].astype(F32)[:40]
        return total.astype(BF)

    x2, y2, zs = [], [], []
    for n, (a, b) in enumerate(CHUNKS):
        cols, span = slice(a * 128, b * 128), pl.ds(a * 128, (b - a) * 128)
        first_sum(0, gx, rx, xs[3 * n : 3 * n + 3], cols)
        x2.append(second_send(0, y, s2x, r2x, at_y, cols, span))
        first_sum(1, gy, ry, ys[3 * n : 3 * n + 3], cols)
        y2.append(second_send(1, x, s2y, r2y, at_x, cols, span))


    slot = lax.broadcasted_iota(jnp.int32, (128, 1), 0)
    sz, sk = slot >> 4, slot & 7
    source = jnp.where(sk < 5, ((slot >> 3) & 1) * 40 + sz * 5 + sk, -1)
    place = (source == lax.broadcasted_iota(jnp.int32, (1, 80), 1)).astype(F32).astype(BF)
    for n, (a, b) in enumerate(CHUNKS):
        cols, span = slice(a * 128, b * 128), pl.ds(a * 128, (b - a) * 128)
        tx = second_sum(0, y, r2x, x2[n], cols)
        ty = second_sum(1, x, r2y, y2[n], cols)
        spread = nn(place[:, :40], tx) + nn(place[:, 40:], ty)
        s3[:, :, cols] = spread.astype(BF).reshape(8, 16, cols.stop - cols.start)
        zs.append([send(s3.at[(z + d) % 8, :, span], r3.at[d - 1, :, span], at_z(d)) for d in FAR])
    for n, (a, b) in enumerate(CHUNKS):
        cols = slice(a * 128, b * 128)
        total = s3[z, :, cols].astype(F32)
        for d, copy in zip(FAR, zs[n]):
            copy.wait_recv()
            total = total + r3[d - 1, :, cols].astype(F32)
        grad_v[:, cols] = total[:5]
        grad_v[:, INNER + a * 128 : INNER + b * 128] = total[8:13]

    grad_out = pltpu.make_async_copy(grad_v, grad_o, load_sem.at[9])
    grad_out.start()
    grad_out.wait()
    block_out.wait()
    back_out.wait()
    for copy in started:
        copy.wait_send()


def finish(a, b, c, a_out, b_out, c_out, a_v, b_v, c_v, sem):
    trio = ((a, a_v, a_out), (b, b_v, b_out), (c, c_v, c_out))
    reads = [pltpu.make_async_copy(t[0], t[1], sem.at[0, i]) for i, t in enumerate(trio)]
    writes = [pltpu.make_async_copy(t[1], t[2], sem.at[1, i]) for i, t in enumerate(trio)]
    for copy in reads:
        copy.start()
    for read, write in zip(reads, writes):
        read.wait()
        write.start()
    for copy in writes:
        copy.wait()


def shards(latents, out_grad, video, owner, w_query, w_key, w_value, w_out):
    hbm = pl.BlockSpec(memory_space=pltpu.HBM)
    deep = 4 * ROWS + 2 * VT
    vm = pltpu.VMEM
    dma = pltpu.SemaphoreType.DMA
    half = ((ROWS, INNER), BF)
    scratch = [
        pltpu.SMEM((1,), jnp.int32), vm((ROWS, D), BF), vm((ROWS, D), BF),
        vm((D, INNER), BF), vm((D, INNER), BF), vm((D, INNER), BF), vm((INNER, D), BF),
        vm((ROWS, D), BF), vm((ROWS, D), BF), vm((5, D), F32),
        vm((ROWS, D), F32), vm((deep, D), BF),
        vm(*half), vm((KEYS, INNER), BF), vm((KEYS, INNER), BF), vm(*half),
        vm((NF, 16, 1024), BF), vm((NF, 16, 1024), BF), vm((NF, 16, 1024), BF), vm((NF, 16, 1024), BF),
        vm((8, 2, VT, D), BF), vm((8, VT, D), BF), vm((8, VT, D), BF), vm((8, VT, D), BF),
        vm((ROWS, INNER), F32), vm(*half), vm(*half), vm((2, deep, INNER), BF),
        vm((2, INNER, D), BF), vm((2, INNER, deep), BF),
        vm((4, 160, INNER), BF), vm((4, 160, INNER), BF), vm((3, 160, INNER), BF), vm((3, 160, INNER), BF),
        vm((4, 48, INNER), BF), vm((4, 48, INNER), BF), vm((3, 48, INNER), BF), vm((3, 48, INNER), BF),
        vm((2, 160, INNER), F32), vm((8, 16, INNER), BF), vm((7, 16, INNER), BF),
        dma((11,)), dma((1, NF)), dma((1, NF)), dma((1, NF)), dma((1, NF)), dma((80,)), dma((80,)),
    ]
    block, back, grads = pl.pallas_call(
        kernel,
        out_shape=(
            jax.ShapeDtypeStruct((ROWS, D), BF),
            jax.ShapeDtypeStruct((ROWS, D), BF),
            jax.ShapeDtypeStruct((5, D), F32),
        ),
        in_specs=[hbm] * 8,
        out_specs=(hbm, hbm, hbm),
        scratch_shapes=scratch,
        compiler_params=pltpu.CompilerParams(
            collective_id=0, has_side_effects=True, vmem_limit_bytes=62 * 1024 * 1024
        ),
    )(
        latents.reshape(ROWS, D),
        out_grad.reshape(ROWS, D),
        video.reshape(8, 2, VT, D),
        owner,
        w_query,
        w_key,
        w_value,
        w_out,
    )
    block, back, grads = pl.pallas_call(
        finish,
        out_shape=(
            jax.ShapeDtypeStruct((ROWS, D), BF),
            jax.ShapeDtypeStruct((ROWS, D), BF),
            jax.ShapeDtypeStruct((5, D), F32),
        ),
        in_specs=[hbm] * 3,
        out_specs=[hbm] * 3,
        scratch_shapes=[vm((ROWS, D), BF), vm((ROWS, D), BF), vm((5, D), F32), dma((2, 3))],
        compiler_params=pltpu.CompilerParams(vmem_limit_bytes=62 * 1024 * 1024),
    )(block, back, grads)
    return block.reshape(latents.shape), back.reshape(latents.shape), grads


def solution(mesh):
    tokens = P("dp", "frame", None, None, None)
    return jax.shard_map(
        shards,
        mesh=mesh,
        in_specs=(tokens, tokens, tokens, P("dp"), P(), P(), P(), P()),
        out_specs=(tokens, tokens, P(("dp", "frame"), None)),
        check_vma=False,
    )
```

```python
import jax
import jax.numpy as jnp
from jax import lax
from jax.experimental import pallas as pl
from jax.experimental.pallas import tpu as pltpu
from jax.sharding import PartitionSpec as P

MESH = pl.DeviceIdType.MESH
BF = jnp.bfloat16
F32 = jnp.float32
D, INNER, HD = 1280, 640, 64
ROWS, VT, NF = 128, 32, 16
KEYS = 256
EPS = 1e-6
CHUNKS = ((0, 3), (3, 5))
TURNS = tuple(range(1, 16))
SLOTS = (4, 3, 5, 2, 6, 1, 7, 0)
ORDER = (2, 1, 3)
FAR = (4, 3, 5, 2, 6, 1, 7)


def nn(a, b):
    return jnp.dot(a, b, preferred_element_type=F32)


def nt(a, b):
    return lax.dot_general(a, b, (((1,), (1,)), ((), ())), preferred_element_type=F32)


def tn(a, b):
    return lax.dot_general(a, b, (((0,), (0,)), ((), ())), preferred_element_type=F32)


def attend(q, k, v, go, mask):
    lane = lax.broadcasted_iota(jnp.int32, (1, 128), 1)
    first = (lane < HD).astype(F32).astype(BF)
    second = (lane >= HD).astype(F32).astype(BF)
    qm = jnp.concatenate([q * first, q * second], axis=0)
    gm = jnp.concatenate([go * first, go * second], axis=0)
    km = jnp.concatenate([k * first, k * second], axis=0)
    vm = jnp.concatenate([v * first, v * second], axis=0)
    e = jnp.where(mask, jnp.exp(nt(qm, k) * 0.125), 0.0)
    dp = nt(gm, v)
    r = 1.0 / jnp.sum(e, axis=1, keepdims=True)
    eb = e.astype(BF)
    o = nn(jnp.concatenate([eb[:ROWS], eb[ROWS:]], axis=1), vm)
    o = o * jnp.where(lane < HD, r[:ROWS], r[ROWS:])
    delta = jnp.sum(gm.astype(F32) * jnp.concatenate([o, o], axis=0), axis=1, keepdims=True)
    p = e * r
    ds = (p * (dp - delta)).astype(BF)
    dq = nn(jnp.concatenate([ds[:ROWS], ds[ROWS:]], axis=1), km) * 0.125
    dk = tn(ds, qm) * 0.125
    dv = tn(p.astype(BF), gm)
    return o, dq, dk, dv


def fold(left, right):
    n, m = left.shape[1], right.shape[1]
    if m < n:
        right = jnp.concatenate([right, jnp.zeros((ROWS, n - m), F32)], axis=1)
    return jnp.concatenate([left.reshape(NF, 8, n), right.reshape(NF, 8, n)], axis=1).astype(BF)


def unfold(block, m):
    wide = block.astype(F32)
    n = wide.shape[2]
    return jnp.concatenate([wide[:, :8].reshape(ROWS, n), wide[:, 8:, :m].reshape(ROWS, m)], axis=1)


def kernel(
    lat, ogr, vid, own, wq_h, wk_h, wv_h, wo_h,
    block_h, back_h, grad_o,
    lat_v, ogr_v, wq, wk, wv, wo, block_v, back_v, grad_v,
    normed, xt, q_v, kk, vv, go_v, sx, sg, ax, ag, so, sd, ro, rd,
    va, vb, vs, vr, ov, dqv, dqt, dkv,
    pt, xp, gx, gy, rx, ry, s2x, s2y, r2x, r2y, m1, s3, r3,
    load_sem, as1, ar1, as2, ar2, ms, mr,
):
    dp = lax.axis_index("dp")
    me = lax.axis_index("frame")
    z, x_lo = dp // 2, dp % 2
    x_hi, y, c = me // 8, (me // 2) % 4, me % 2
    x = x_hi * 2 + x_lo

    def at_x(d):
        to = (x + d) % 4
        return (z * 2 + to % 2, (to // 2) * 8 + y * 2 + c)

    def at_y(d):
        return (dp, x_hi * 8 + ((y + d) % 4) * 2 + c)

    def at_z(d):
        return (((z + d) % 8) * 2 + x_lo, me)

    def at_f(d):
        return (dp, (me + d) % NF)

    pair = (dp, me + 1 - 2 * c)

    loads = [
        pltpu.make_async_copy(src, dst, load_sem.at[i])
        for i, (src, dst) in enumerate(
            [(lat, lat_v), (ogr, ogr_v), (wo_h, wo), (wq_h, wq), (wk_h, wk), (wv_h, wv), (vid.at[:, c], va)]
        )
    ]
    loads[0].start()

    barrier = pltpu.get_barrier_semaphore()
    peers = [at_f(d) for d in range(1, NF)] + [at_x(1), at_x(3)] + [at_z(d) for d in range(1, 8)]
    for peer in peers:
        pl.semaphore_signal(barrier, inc=1, device_id=peer, device_id_type=MESH)
    for copy in loads[1:]:
        copy.start()

    count = [0]
    started = []

    def send(src, dst, peer, ss=None, rs=None):
        if ss is None:
            ss, rs = ms.at[count[0]], mr.at[count[0]]
            count[0] += 1
        copy = pltpu.make_async_remote_copy(
            src_ref=src, dst_ref=dst, send_sem=ss, recv_sem=rs, device_id=peer, device_id_type=MESH
        )
        copy.start()
        started.append(copy)
        return copy

    def scatter(src, dst, ss, rs):
        for d in TURNS:
            send(src.at[(me + d) % NF], dst.at[me], at_f(d), ss.at[d], rs.at[d])

    def gathered(src, dst, rs):
        dst[me] = src[me]
        for d in TURNS:
            slot = dst.at[(me + NF - d) % NF]
            pltpu.make_async_remote_copy(
                src_ref=slot, dst_ref=slot, send_sem=rs.at[d], recv_sem=rs.at[d], device_id=pair, device_id_type=MESH
            ).wait_recv()

    def to_pair(ref, row, rows, cols=None):
        if cols is None:
            return send(ref.at[pl.ds(row, rows)], ref.at[pl.ds(row + rows, rows)], pair)
        return send(ref.at[:, pl.ds(row, rows), cols], ref.at[:, pl.ds(row + rows, rows), cols], pair)

    loads[0].wait()
    xf = lat_v[...].astype(F32)
    factor = lax.rsqrt(jnp.mean(xf * xf, axis=1, keepdims=True) + EPS)
    norm = xf * factor
    normed[...] = norm
    xt[:ROWS] = norm.astype(BF)
    sx[...] = fold(norm[:, :INNER], norm[:, INNER:])
    loads[1].wait()
    loads[2].wait()
    gf = nt(ogr_v[...], wo[...])
    sg[...] = fold(gf[:, :384], gf[:, 384:])
    go_v[...] = gf.astype(BF)

    pl.semaphore_wait(barrier, len(peers))
    core_copies = [send(vid.at[(me // 2 + d) % 8, 1 - c], vb.at[d], pair) for d in SLOTS]
    scatter(sx, ax, as1.at[0], ar1.at[0])
    scatter(sg, ag, as1.at[1], ar1.at[1])
    xn_copy = to_pair(xt, 0, ROWS)

    for copy in loads[3:6]:
        copy.wait()
    xn = xt[:ROWS]
    q_v[...] = nn(xn, wq[...]).astype(BF)
    kk[:ROWS] = nn(xn, wk[...]).astype(BF)
    vv[:ROWS] = nn(xn, wv[...]).astype(BF)

    who = own[0]
    loads[6].wait()
    w = (who % 2 == c).astype(F32)
    video_copies = {}
    for copy, d in zip(core_copies, SLOTS):
        copy.wait_recv()
        to = (me // 2 + d) % 8
        vs[d] = (va[to].astype(F32) * w + vb[d].astype(F32) * (1.0 - w)).astype(BF)
        if d:
            video_copies[d] = send(vs.at[d], vr.at[d], (dp, to * 2 + c))

    new = lax.broadcasted_iota(jnp.int32, (INNER, 1), 0)
    u = (new * 52429) >> 18
    k5 = new - 5 * u
    uz, lo, hi = u & 7, (u >> 3) & 3, u >> 5
    column = lax.broadcasted_iota(jnp.int32, (1, D), 1)

    def one_hot(ux, uy):
        old = ((((uz * 2 + (ux & 1)) * 2 + (ux >> 1)) * 4 + uy) * 2 + c) * 5 + k5
        return (old == column).astype(F32).astype(BF)

    pt[0] = one_hot(hi, lo)
    pt[1] = one_hot(lo, hi)

    def permute(first, last):
        rows = xt[first:last]
        for i in range(2):
            xp[i, :, first:last] = nt(pt[i], rows).astype(BF)

    gathered(sx, ax, ar1.at[0])
    xa = unfold(ax[...], INNER).astype(BF)
    xt[2 * ROWS : 3 * ROWS] = xa
    xa_copy = to_pair(xt, 2 * ROWS, ROWS)
    qa = nn(xa, wq[...]).astype(BF)
    ka = nn(xa, wk[...]).astype(BF)
    va_t = nn(xa, wv[...]).astype(BF)
    same = (
        (lax.broadcasted_iota(jnp.int32, (2 * ROWS, ROWS), 0) - lax.broadcasted_iota(jnp.int32, (2 * ROWS, ROWS), 1)) & 7
    ) == 0
    gathered(sg, ag, ar1.at[1])
    ga = unfold(ag[...], 256).astype(BF)
    outs = []
    for p in range(5):
        cols = slice(p * 128, (p + 1) * 128)
        o, dq, dk, dv = attend(qa[:, cols], ka[:, cols], va_t[:, cols], ga[:, cols], same)
        outs.append(o)
        dqt[:, cols] = dq.astype(BF)
        dkv[0, 2 * ROWS : 3 * ROWS, cols] = dk.astype(BF)
        dkv[1, 2 * ROWS : 3 * ROWS, cols] = dv.astype(BF)
    so[...] = fold(jnp.concatenate(outs[:3], axis=1), jnp.concatenate(outs[3:], axis=1))
    dn = nt(dqt[...], wq[...]) + nt(dkv[0, 2 * ROWS : 3 * ROWS], wk[...]) + nt(dkv[1, 2 * ROWS : 3 * ROWS], wv[...])
    sd[...] = fold(dn[:, :INNER], dn[:, INNER:])
    scatter(sd, rd, as2.at[0], ar2.at[0])
    scatter(so, ro, as2.at[1], ar2.at[1])
    dt_copy = to_pair(dkv, 2 * ROWS, ROWS, pl.ds(0, INNER))

    xn_copy.wait_recv()
    permute(0, 2 * ROWS)
    xa_copy.wait_recv()
    permute(2 * ROWS, 4 * ROWS)

    cond = vs[0].astype(F32) * (who // 2 == me // 2).astype(F32)
    for d in SLOTS:
        if d:
            video_copies[d].wait_recv()
            cond = cond + vr[d].astype(F32) * (who // 2 == (me // 2 + 8 - d) % 8).astype(F32)
    cn = (cond * lax.rsqrt(jnp.mean(cond * cond, axis=1, keepdims=True) + EPS)).astype(BF)
    xt[4 * ROWS : 4 * ROWS + VT] = cn
    cn_copy = to_pair(xt, 4 * ROWS, VT)
    zeros = jnp.zeros((KEYS - ROWS - VT, INNER), BF)
    kk[ROWS : ROWS + VT] = nn(cn, wk[...]).astype(BF)
    vv[ROWS : ROWS + VT] = nn(cn, wv[...]).astype(BF)
    kk[ROWS + VT :] = zeros
    vv[ROWS + VT :] = zeros
    real = lax.broadcasted_iota(jnp.int32, (2 * ROWS, KEYS), 1) < ROWS + VT
    late = []
    for a, b in CHUNKS:
        for p in range(a, b):
            cols = slice(p * 128, (p + 1) * 128)
            o, dq, dk, dv = attend(q_v[:, cols], kk[:, cols], vv[:, cols], go_v[:, cols], real)
            ov[:, cols] = o
            dqv[:, cols] = dq.astype(BF)
            for i, t in enumerate((dk.astype(BF), dv.astype(BF))):
                dkv[i, :ROWS, cols] = t[:ROWS]
                dkv[i, 4 * ROWS : 4 * ROWS + VT, cols] = t[ROWS : ROWS + VT]
        span = pl.ds(a * 128, (b - a) * 128)
        late.append((to_pair(dkv, 0, ROWS, span), to_pair(dkv, 4 * ROWS, VT, span)))
    cn_copy.wait_recv()
    permute(4 * ROWS, 4 * ROWS + 2 * VT)
    dt_copy.wait_recv()

    xs, ys = [], []
    for n, (a, b) in enumerate(CHUNKS):
        cols = slice(a * 128, b * 128)
        span = pl.ds(a * 128, (b - a) * 128)
        for copy in late[n]:
            copy.wait_recv()
        for d in (2, 1, 3, 0):
            bx = pl.multiple_of(((x + d) % 4) * 160, 32)
            gx[d, :, cols] = nn(xp[0, pl.ds(bx, 160), :], dkv[0, :, cols]).astype(BF)
            if d:
                xs.append(send(gx.at[d, :, span], rx.at[d - 1, :, span], at_x(d)))
            by = pl.multiple_of(((y + d) % 4) * 160, 32)
            gy[d, :, cols] = nn(xp[1, pl.ds(by, 160), :], dkv[1, :, cols]).astype(BF)
            if d:
                ys.append(send(gy.at[d, :, span], ry.at[d - 1, :, span], at_y(d)))

    gathered(so, ro, ar2.at[1])
    hidden = (ov[...] + unfold(ro[...], 256)).astype(BF)
    block_v[...] = (lat_v[...].astype(F32) + nn(hidden, wo[...])).astype(BF)
    block_out = pltpu.make_async_copy(block_v, block_h, load_sem.at[7])
    block_out.start()
    gathered(sd, rd, ar2.at[0])
    dn = nt(dqv[...], wq[...]) + nt(dkv[0, :ROWS], wk[...]) + nt(dkv[1, :ROWS], wv[...]) + unfold(rd[...], INNER)
    norm = normed[...]
    xf = lat_v[...].astype(F32)
    factor = lax.rsqrt(jnp.mean(xf * xf, axis=1, keepdims=True) + EPS)
    back = ogr_v[...].astype(F32) + factor * (dn - norm * jnp.mean(dn * norm, axis=1, keepdims=True))
    back_v[...] = back.astype(BF)
    back_out = pltpu.make_async_copy(back_v, back_h, load_sem.at[8])
    back_out.start()

    def first_sum(at, g, r, copies, cols):
        total = g[0, :, cols].astype(F32)
        for i, copy in enumerate(copies):
            copy.wait_recv()
            total = total + r[ORDER[i] - 1, :, cols].astype(F32)
        m1[at, :, cols] = total

    def second_send(at, position, s2, r2, peer, cols, span):
        pad = jnp.zeros((8, cols.stop - cols.start), F32)
        copies = []
        for d in ORDER:
            rows = pl.multiple_of(((position + d) % 4) * 40, 8)
            s2[d, :, cols] = jnp.concatenate([m1[at, pl.ds(rows, 40), cols], pad], axis=0).astype(BF)
            copies.append(send(s2.at[d, :, span], r2.at[d - 1, :, span], peer(d)))
        return copies

    def second_sum(at, position, r2, copies, cols):
        total = m1[at, pl.ds(pl.multiple_of(position * 40, 8), 40), cols]
        for i, copy in enumerate(copies):
            copy.wait_recv()
            total = total + r2[ORDER[i] - 1, :, cols].astype(F32)[:40]
        return total.astype(BF)

    x2, y2, zs = [], [], []
    for n, (a, b) in enumerate(CHUNKS):
        cols, span = slice(a * 128, b * 128), pl.ds(a * 128, (b - a) * 128)
        first_sum(0, gx, rx, xs[3 * n : 3 * n + 3], cols)
        x2.append(second_send(0, y, s2x, r2x, at_y, cols, span))
        first_sum(1, gy, ry, ys[3 * n : 3 * n + 3], cols)
        y2.append(second_send(1, x, s2y, r2y, at_x, cols, span))

    slot = lax.broadcasted_iota(jnp.int32, (128, 1), 0)
    sz, sk = slot >> 4, slot & 7
    source = jnp.where(sk < 5, ((slot >> 3) & 1) * 40 + sz * 5 + sk, -1)
    place = (source == lax.broadcasted_iota(jnp.int32, (1, 80), 1)).astype(F32).astype(BF)
    for n, (a, b) in enumerate(CHUNKS):
        cols, span = slice(a * 128, b * 128), pl.ds(a * 128, (b - a) * 128)
        tx = second_sum(0, y, r2x, x2[n], cols)
        ty = second_sum(1, x, r2y, y2[n], cols)
        spread = nn(place[:, :40], tx) + nn(place[:, 40:], ty)
        s3[:, :, cols] = spread.astype(BF).reshape(8, 16, cols.stop - cols.start)
        zs.append([send(s3.at[(z + d) % 8, :, span], r3.at[d - 1, :, span], at_z(d)) for d in FAR])
    for n, (a, b) in enumerate(CHUNKS):
        cols = slice(a * 128, b * 128)
        total = s3[z, :, cols].astype(F32)
        for d, copy in zip(FAR, zs[n]):
            copy.wait_recv()
            total = total + r3[d - 1, :, cols].astype(F32)
        grad_v[:, cols] = total[:5]
        grad_v[:, INNER + a * 128 : INNER + b * 128] = total[8:13]

    grad_out = pltpu.make_async_copy(grad_v, grad_o, load_sem.at[9])
    grad_out.start()
    grad_out.wait()
    block_out.wait()
    back_out.wait()
    for copy in started:
        copy.wait_send()


def finish(a, b, c, a_out, b_out, c_out, a_v, b_v, c_v, sem):
    trio = ((a, a_v, a_out), (b, b_v, b_out), (c, c_v, c_out))
    reads = [pltpu.make_async_copy(t[0], t[1], sem.at[0, i]) for i, t in enumerate(trio)]
    writes = [pltpu.make_async_copy(t[1], t[2], sem.at[1, i]) for i, t in enumerate(trio)]
    for copy in reads:
        copy.start()
    for read, write in zip(reads, writes):
        read.wait()
        write.start()
    for copy in writes:
        copy.wait()


def shards(latents, out_grad, video, owner, w_query, w_key, w_value, w_out):
    hbm = pl.BlockSpec(memory_space=pltpu.HBM)
    deep = 4 * ROWS + 2 * VT
    vm = pltpu.VMEM
    dma = pltpu.SemaphoreType.DMA
    half = ((ROWS, INNER), BF)
    scratch = [
        vm((ROWS, D), BF), vm((ROWS, D), BF),
        vm((D, INNER), BF), vm((D, INNER), BF), vm((D, INNER), BF), vm((INNER, D), BF),
        vm((ROWS, D), BF), vm((ROWS, D), BF), vm((5, D), F32),
        vm((ROWS, D), F32), vm((deep, D), BF),
        vm(*half), vm((KEYS, INNER), BF), vm((KEYS, INNER), BF), vm(*half),
        vm((NF, 16, INNER), BF), vm((NF, 16, 384), BF), vm((NF, 16, INNER), BF), vm((NF, 16, 384), BF),
        vm((NF, 16, 384), BF), vm((NF, 16, INNER), BF), vm((NF, 16, 384), BF), vm((NF, 16, INNER), BF),
        vm((8, VT, D), BF), vm((8, VT, D), BF), vm((8, VT, D), BF), vm((8, VT, D), BF),
        vm((ROWS, INNER), F32), vm(*half), vm(*half), vm((2, deep, INNER), BF),
        vm((2, INNER, D), BF), vm((2, INNER, deep), BF),
        vm((4, 160, INNER), BF), vm((4, 160, INNER), BF), vm((3, 160, INNER), BF), vm((3, 160, INNER), BF),
        vm((4, 48, INNER), BF), vm((4, 48, INNER), BF), vm((3, 48, INNER), BF), vm((3, 48, INNER), BF),
        vm((2, 160, INNER), F32), vm((8, 16, INNER), BF), vm((7, 16, INNER), BF),
        dma((10,)), dma((2, NF)), dma((2, NF)), dma((2, NF)), dma((2, NF)), dma((80,)), dma((80,)),
    ]
    block, back, grads = pl.pallas_call(
        kernel,
        out_shape=(
            jax.ShapeDtypeStruct((ROWS, D), BF),
            jax.ShapeDtypeStruct((ROWS, D), BF),
            jax.ShapeDtypeStruct((5, D), F32),
        ),
        in_specs=[hbm, hbm, hbm, pl.BlockSpec(memory_space=pltpu.SMEM)] + [hbm] * 4,
        out_specs=(hbm, hbm, hbm),
        scratch_shapes=scratch,
        compiler_params=pltpu.CompilerParams(
            collective_id=0, has_side_effects=True, vmem_limit_bytes=62 * 1024 * 1024
        ),
    )(
        latents.reshape(ROWS, D),
        out_grad.reshape(ROWS, D),
        video.reshape(8, 2, VT, D),
        owner,
        w_query,
        w_key,
        w_value,
        w_out,
    )
    block, back, grads = pl.pallas_call(
        finish,
        out_shape=(
            jax.ShapeDtypeStruct((ROWS, D), BF),
            jax.ShapeDtypeStruct((ROWS, D), BF),
            jax.ShapeDtypeStruct((5, D), F32),
        ),
        in_specs=[hbm] * 3,
        out_specs=[hbm] * 3,
        scratch_shapes=[vm((ROWS, D), BF), vm((ROWS, D), BF), vm((5, D), F32), dma((2, 3))],
        compiler_params=pltpu.CompilerParams(vmem_limit_bytes=62 * 1024 * 1024),
    )(block, back, grads)
    return block.reshape(latents.shape), back.reshape(latents.shape), grads


def solution(mesh):
    tokens = P("dp", "frame", None, None, None)
    return jax.shard_map(
        shards,
        mesh=mesh,
        in_specs=(tokens, tokens, tokens, P("dp"), P(), P(), P(), P()),
        out_specs=(tokens, tokens, P(("dp", "frame"), None)),
        check_vma=False,
    )
```
